32 devices in a mesh: dp: 8 (over z, y), seq: 4 (over x, core).
Axes of the slice: x: 2, y: 2, z: 4, core: 2. Of those that a mesh axis runs over, the one named last changes fastest.
Arguments:
- layer_input: bfloat16 [8, 1024, 768], P('dp', 'seq'), may hold values from -6 to 6
- segments: int32 [8, 1024], P('dp', 'seq'), may hold values from 0 to 4, as said below
- cotangent: bfloat16 [8, 1024, 768], P('dp', 'seq'), may hold values from -6 to 6
- attend_weight: bfloat16 [768, 2304], P(('dp', 'seq')), may hold values from -0.21875 to 0.21875
- query_bias: bfloat16 [768], P(('dp', 'seq')), may hold values from -3 to 3
- value_bias: bfloat16 [768], P(('dp', 'seq')), may hold values from -3 to 3
- merge_weight: bfloat16 [768, 768], P(('dp', 'seq')), may hold values from -0.875 to 0.875
- merge_bias: bfloat16 [768], P(('dp', 'seq')), may hold values from -3 to 3
- first_gain: bfloat16 [768], P(('dp', 'seq')), may hold values from 0.5 to 1.5
- first_shift: bfloat16 [768], P(('dp', 'seq')), may hold values from -2 to 2
- expand_weight: bfloat16 [768, 3072], P(('dp', 'seq')), may hold values from -0.21875 to 0.21875
- expand_bias: bfloat16 [3072], P(('dp', 'seq')), may hold values from -3 to 3
- shrink_weight: bfloat16 [3072, 768], P(('dp', 'seq')), may hold values from -0.109375 to 0.109375
- shrink_bias: bfloat16 [768], P(('dp', 'seq')), may hold values from -3 to 3
- second_gain: bfloat16 [768], P(('dp', 'seq')), may hold values from 0.5 to 1.5
- second_shift: bfloat16 [768], P(('dp', 'seq')), may hold values from -2 to 2
Outputs:
- layer_output: bfloat16 [8, 1024, 768], P('dp', 'seq')
- input_grad: float32 [8, 1024, 768], P('dp', 'seq')
- attend_grad: float32 [768, 2304], P(('dp', 'seq'))
- querybias_grad: float32 [768], P(('dp', 'seq'))
- valuebias_grad: float32 [768], P(('dp', 'seq'))
- merge_grad: float32 [768, 768], P(('dp', 'seq'))
- mergebias_grad: float32 [768], P(('dp', 'seq'))
- firstgain_grad: float32 [768], P(('dp', 'seq'))
- firstshift_grad: float32 [768], P(('dp', 'seq'))
- expand_grad: float32 [768, 3072], P(('dp', 'seq'))
- expandbias_grad: float32 [3072], P(('dp', 'seq'))
- shrink_grad: float32 [3072, 768], P(('dp', 'seq'))
- shrinkbias_grad: float32 [768], P(('dp', 'seq'))
- secondgain_grad: float32 [768], P(('dp', 'seq'))
- secondshift_grad: float32 [768], P(('dp', 'seq'))
The draws below stay inside these ranges and needn't reach their ends.
Inputs may be any that keep to these rules, and one draw needn't show every extreme that they name: `segments`: segment numbers are 0 at the first token of every sequence, never fall along it, and are 4 at its last token. Of the 1 sequence on each index of dp, one, drawn from the seed, holds a document that starts within its first 256 tokens and ends within its last 256 tokens.
All inputs are finite; a program needn't handle non-finite values.
Results may differ from the reference program's by a relative error of at most 0.018.
Values may be sent and summed in bfloat16 or wider, within the bound.
A program may use at most 128 MiB of HBM per device.

```python
import jax
import jax.numpy as jnp
from jax import lax

D = 768
H = 12
HD = 64
FF = 3072
GROUP = 256
SEQ_DEV = 1
BOUNDS = 4
SEQS = 8
LENGTH = 1024


def draw_segments(key, part):
    key = jax.random.fold_in(key, 11)
    keys_split = jax.random.split(key, 4)
    spread_bounds = jax.random.randint(keys_split[0], (SEQS, BOUNDS), 1, LENGTH)
    early_bounds = jax.random.randint(keys_split[1], (SEQS, BOUNDS), 1, GROUP)
    late_bounds = jax.random.randint(keys_split[2], (SEQS, BOUNDS), LENGTH - GROUP + 1, LENGTH)
    chosen = jax.random.randint(keys_split[3], (SEQS // SEQ_DEV, 1), 0, SEQ_DEV)
    slots = jnp.arange(SEQS, dtype=jnp.int32).reshape(SEQS // SEQ_DEV, SEQ_DEV)
    spanning = (slots % SEQ_DEV == chosen).reshape(SEQS)
    halves = jnp.arange(BOUNDS, dtype=jnp.int32) < BOUNDS // 2
    framed = jnp.where(halves[None, :], early_bounds, late_bounds)
    bounds_all = jnp.where(spanning[:, None], framed, spread_bounds)
    places = jnp.arange(LENGTH, dtype=jnp.int32)
    return jnp.sum((bounds_all[:, :, None] <= places[None, None, :]).astype(jnp.int32), axis=1)


def with_spikes(values, stream_key, source, target, blocks, factor):
    def block_of(dim):
        return (jnp.arange(values.shape[dim]) // (values.shape[dim] // blocks)).reshape((-1,) + (1,) * (values.ndim - 1 - dim))

    near = jax.random.permutation(stream_key, blocks)[block_of(target)]
    other_side = (block_of(target) + blocks // 2) % blocks
    return jnp.where((block_of(source) == near) | (block_of(source) == other_side), factor * values, values)


def block_scale(stream_key, extent, pieces, smallest, high):
    gain, own = 1.0, jax.random.fold_in(stream_key, 6)
    for dim, shards_of in pieces:
        draws = jnp.exp(jax.random.uniform(jax.random.fold_in(own, dim), (shards_of,), jnp.float32, smallest / len(pieces), high / len(pieces)))
        gain = gain * jnp.repeat(draws, extent[dim] // shards_of).reshape([-1 if axis == dim else 1 for axis in range(len(extent))])
    return gain


def normal_values(rng, dims, deviation, reach, shards=(), kind=jnp.bfloat16):
    values = jax.random.normal(rng, dims, jnp.float32) * deviation
    if len(shards) > 0:
        values = block_scale(rng, dims, shards, -0.22, 0.18) * values
    return jnp.clip(values, min=-reach, max=reach).astype(kind)


def bell_draw_with(stream_key, shape, deviation, bound, pieces, heavy, kind=jnp.bfloat16):
    values = deviation * jax.random.normal(stream_key, shape, jnp.float32)
    if pieces:
        values = values * block_scale(stream_key, shape, pieces, -0.22, 0.18)
    return jnp.clip(with_spikes(values, jax.random.fold_in(stream_key, 3), *heavy), -bound, bound).astype(kind)


def setup_inputs(seed: int = 0) -> dict:
    key_list = jax.random.split(jax.random.key(seed), 17)
    layer_input = normal_values(key_list[0], (SEQS, LENGTH, D), 1.0, 6.0, ((0, 8), (1, 4)))
    segments = draw_segments(jax.random.fold_in(key_list[16], 71), 0)
    cotangent = bell_draw_with(key_list[2], (SEQS, LENGTH, D), 1.0, 6.0, ((0, 8), (1, 4)), (1, 2, 4, 2.0))
    attend_weight = normal_values(key_list[3], (D, 3 * D), D ** -0.5, 0.21875, ((0, 32),))
    query_bias = normal_values(key_list[4], (D,), 0.5, 3.0, ((0, 32),))
    value_bias = normal_values(key_list[5], (D,), 0.5, 3.0, ((0, 32),))
    merge_weight = normal_values(key_list[6], (D, D), (D // 16) ** -0.5, 0.875, ((0, 32),))
    merge_bias = normal_values(key_list[7], (D,), 0.5, 3.0, ((0, 32),))
    first_gain = jnp.clip(1.0 + 0.1 * jax.random.normal(key_list[8], (D,), jnp.float32), 0.5, 1.5).astype(jnp.bfloat16)
    first_shift = normal_values(key_list[9], (D,), 0.3, 2.0, ((0, 32),))
    expand_weight = normal_values(key_list[10], (D, FF), D ** -0.5, 0.21875, ((0, 32),))
    expand_bias = normal_values(key_list[11], (FF,), 0.5, 3.0, ((0, 32),))
    shrink_weight = normal_values(key_list[12], (FF, D), FF ** -0.5, 0.109375, ((0, 32),))
    shrink_bias = normal_values(key_list[13], (D,), 0.5, 3.0, ((0, 32),))
    second_gain = jnp.clip(1.0 + 0.1 * jax.random.normal(key_list[14], (D,), jnp.float32), 0.5, 1.5).astype(jnp.bfloat16)
    second_shift = normal_values(key_list[15], (D,), 0.3, 2.0, ((0, 32),))
    return dict(layer_input=layer_input, segments=segments, cotangent=cotangent, attend_weight=attend_weight, query_bias=query_bias, value_bias=value_bias, merge_weight=merge_weight, merge_bias=merge_bias, first_gain=first_gain, first_shift=first_shift, expand_weight=expand_weight, expand_bias=expand_bias, shrink_weight=shrink_weight, shrink_bias=shrink_bias, second_gain=second_gain, second_shift=second_shift)


EPSILON = 1e-05
MASKED = -1e+30
QUERY_SCALE = 0.125
PRECISE = lax.Precision.HIGHEST

@jax.custom_vjp
def low(v):
    return lax.optimization_barrier(v.astype(jnp.bfloat16)).astype(jnp.float32)

@jax.custom_vjp
def low_back(v):
    return v

def low_keep(v):
    return (low(v), None)

def low_pass(kept, grad):
    return (grad,)

def back_keep(v):
    return (v, None)

def back_low(kept, grad):
    return (low(grad),)
low.defvjp(low_keep, low_pass)
low_back.defvjp(back_keep, back_low)

def normalize(values, gain_vec, shift_vec):
    centred = values - lax.optimization_barrier(jnp.mean(values, axis=-1, keepdims=True))
    variance = lax.optimization_barrier(jnp.mean(centred * centred, axis=-1, keepdims=True))
    return centred * lax.rsqrt(variance + EPSILON) * gain_vec + shift_vec

def decoder_layer(inputs, labels, params):
    attend_weight, query_bias, value_bias, merge_weight, merge_bias, first_gain, first_shift, expand_weight, expand_bias, shrink_weight, shrink_bias, second_gain, second_shift = params
    first_normed = low(normalize(inputs, first_gain, first_shift))
    project = jnp.dot(first_normed, attend_weight, precision=PRECISE)
    queries = low(low_back((project[:, :D] + query_bias) * QUERY_SCALE))
    key_rows = low(low_back(project[:, D:2 * D]))
    value_rows = low(low_back(project[:, 2 * D:] + value_bias))
    query_heads = queries.reshape(LENGTH, H, HD)
    key_heads = key_rows.reshape(LENGTH, H, HD)
    value_heads = value_rows.reshape(LENGTH, H, HD)
    scores = low_back(jnp.einsum('qhd,khd->hqk', query_heads, key_heads, precision=PRECISE))
    places = jnp.arange(LENGTH, dtype=jnp.int32)
    allowed = (places[None, :] <= places[:, None]) & (labels[None, :] == labels[:, None])
    masked = jnp.where(allowed[None], scores, MASKED)
    highest = lax.optimization_barrier(jnp.max(masked, axis=-1, keepdims=True))
    raised = jnp.where(allowed[None], jnp.exp(masked - highest), 0.0)
    probs = raised / lax.optimization_barrier(jnp.sum(raised, axis=-1, keepdims=True))
    mixed = jnp.einsum('hqk,khd->qhd', low(probs), value_heads, precision=PRECISE).reshape(LENGTH, D)
    mixed = low(low_back(mixed))
    residual = inputs + low_back(jnp.dot(mixed, merge_weight, precision=PRECISE) + merge_bias)
    second_normed = low(normalize(residual, second_gain, second_shift))
    hidden_pre = low_back(jnp.dot(second_normed, expand_weight, precision=PRECISE) + expand_bias)
    hidden = low(jax.nn.gelu(hidden_pre))
    return residual + jnp.dot(hidden, shrink_weight, precision=PRECISE) + shrink_bias

def reference(layer_input, segments, cotangent, attend_weight, query_bias, value_bias, merge_weight, merge_bias, first_gain, first_shift, expand_weight, expand_bias, shrink_weight, shrink_bias, second_gain, second_shift):
    params = tuple((item.astype(jnp.float32) for item in (attend_weight, query_bias, value_bias, merge_weight, merge_bias, first_gain, first_shift, expand_weight, expand_bias, shrink_weight, shrink_bias, second_gain, second_shift)))

    def per_sequence(totals, sequence):
        inputs, labels, upstream = sequence
        result, pullback = jax.vjp(lambda given, weights: decoder_layer(given, labels, weights), inputs.astype(jnp.float32), params)
        grad_inputs, grad_params = pullback(upstream.astype(jnp.float32))
        totals = jax.tree.map(lambda stored, addend: stored + addend, totals, grad_params)
        return (totals, (result.astype(jnp.bfloat16), grad_inputs))
    zero_grads = jax.tree.map(jnp.zeros_like, params)
    totals, (outputs, input_grads) = lax.scan(per_sequence, zero_grads, (layer_input, segments, cotangent))
    return (outputs, input_grads, totals[0], totals[1], totals[2], totals[3], totals[4], totals[5], totals[6], totals[7], totals[8], totals[9], totals[10], totals[11], totals[12])
```

```python
import functools

import jax
import jax.numpy as jnp
from jax import lax
from jax.experimental import pallas as pl
from jax.experimental.pallas import tpu as pltpu
from jax.sharding import PartitionSpec as P

HD = 64
EPSILON = 1e-05
MASKED = -1e30
QUERY_SCALE = 0.125
MESH = pl.DeviceIdType.MESH
VMEM_LIMIT = 58 * 1024 * 1024


def placement(dims):
    big_y = dims[1]
    dp, seq = lax.axis_index("dp"), lax.axis_index("seq")
    return dp // big_y, dp % big_y, seq // 2, seq % 2


def device_of(dims, z, y, x, core):
    return (z * dims[1] + y, x * 2 + core)


def owner_of(dims, z, y, x, core):
    return (z * dims[1] + y) * (2 * dims[2]) + x * 2 + core


def greet(dims, z, y, x, core):
    big_z, big_y, big_x = dims
    barrier = pltpu.get_barrier_semaphore()

    def signal(target):
        pl.semaphore_signal(barrier, inc=1, device_id=target, device_id_type=MESH)

    @pl.when(z > 0)
    def _():
        signal(device_of(dims, z - 1, y, x, core))

    @pl.when(z < big_z - 1)
    def _():
        signal(device_of(dims, z + 1, y, x, core))

    for d in range(1, big_y):
        signal(device_of(dims, z, (y + d) % big_y, x, core))
    for d in range(1, big_x):
        signal(device_of(dims, z, y, (x + d) % big_x, core))
    signal(device_of(dims, z, y, x, 1 - core))
    along_z = (z + big_z - 1) // big_z + (big_z - 1 - z + big_z - 1) // big_z
    pl.semaphore_wait(barrier, big_y - 1 + big_x - 1 + 1 + along_z)


def gather_kernel(
    dims, halves, plan, attend, merge, expand, shrink, vectors, out, src, own_sem,
    z_send, y_send, x_send, c_send, recv, c_recv,
):
    big_z, big_y, big_x = dims
    z, y, x, core = placement(dims)
    me = owner_of(dims, z, y, x, core)
    for k, part in enumerate((attend, merge, expand, shrink, vectors)):
        for first, count, column in plan[k]:
            src[first : first + count, :] = part[:, column : column + src.shape[1]]
    greet(dims, z, y, x, core)
    own = pltpu.make_async_copy(src, out.at[me], own_sem)
    own.start()

    def piece(i, h):
        return out.at[i, pl.ds(*halves[h])]

    def send(i, h, target, send_sem, recv_sem, mine=False):
        pltpu.make_async_remote_copy(
            src_ref=src.at[pl.ds(*halves[h])] if mine else piece(i, h),
            dst_ref=piece(i, h),
            send_sem=send_sem,
            recv_sem=recv_sem,
            device_id=target,
            device_id_type=MESH,
        ).start()

    def arrived(i, h):
        pltpu.make_async_copy(piece(i, h), piece(i, h), recv.at[h, i]).wait()

    def to_y(i, h, mine=False):
        for d in range(1, big_y):
            target = device_of(dims, z, (y + d) % big_y, x, core)
            send(i, h, target, y_send.at[h], recv.at[h, i], mine)

    def to_x(i, h, mine=False):
        for d in range(1, big_x):
            target = device_of(dims, z, y, (x + d) % big_x, core)
            send(i, h, target, x_send.at[h], recv.at[h, i], mine)

    def to_core(i, h, mine=False):
        send(i, h, device_of(dims, z, y, x, 1 - core), c_send.at[h], c_recv.at[h], mine)

    def up(i, h, s, mine=False):
        @pl.when(z < big_z - 1)
        def _():
            send(i, h, device_of(dims, z + 1, y, x, core), z_send.at[h, 0, s], recv.at[h, i], mine)

    def down(i, h, s, mine=False):
        @pl.when(z > 0)
        def _():
            send(i, h, device_of(dims, z - 1, y, x, core), z_send.at[h, 1, s], recv.at[h, i], mine)

    def fan(i, h, mine=False):
        for go in (to_y, to_x) if h == 0 else (to_x, to_y):
            go(i, h, mine)
        to_core(i, h, mine)

    for h in (0, 1):
        up(me, h, 0, True)
        down(me, h, 0, True)
        fan(me, h, True)

    for s in range(1, big_z):
        for h in (0, 1):

            @pl.when(z - s >= 0)
            def _(s=s, h=h):
                i = owner_of(dims, z - s, y, x, core)
                arrived(i, h)
                if s < big_z - 1:
                    up(i, h, s)
                fan(i, h)

            @pl.when(z + s < big_z)
            def _(s=s, h=h):
                i = owner_of(dims, z + s, y, x, core)
                arrived(i, h)
                if s < big_z - 1:
                    down(i, h, s)
                fan(i, h)

    @pl.loop(0, big_z)
    def _(s):
        at = (z + s) % big_z
        for d in range(1, big_y):
            i = owner_of(dims, at, (y + d) % big_y, x, core)
            arrived(i, 0)
            to_x(i, 0)
            to_core(i, 0)
        for d in range(1, big_x):
            i = owner_of(dims, at, y, (x + d) % big_x, core)
            arrived(i, 1)
            to_y(i, 1)
            to_core(i, 1)

    for e in range(max(big_x, big_y)):

        @pl.loop(0, big_z)
        def _(s, e=e):
            at = (z + s) % big_z
            if e < big_y:
                for d in range(1, big_x):
                    i = owner_of(dims, at, (y + e) % big_y, (x + d) % big_x, core)
                    arrived(i, 0)
                    to_core(i, 0)
            if e < big_x:
                for d in range(1, big_y):
                    i = owner_of(dims, at, (y + d) % big_y, (x + e) % big_x, core)
                    arrived(i, 1)
                    to_core(i, 1)

    def drain(count, h, sem):
        if count:
            region = out.at[pl.ds(0, count), pl.ds(*halves[h])]
            pltpu.make_async_copy(region, region, sem).wait()

    own.wait()
    for h in (0, 1):
        drain(big_x * big_y * big_z, h, c_recv.at[h])
        drain(big_x * big_y * big_z, h, c_send.at[h])
        drain((big_y - 1) * big_z * (1 if h == 0 else big_x), h, y_send.at[h])
        drain((big_x - 1) * big_z * (big_y if h == 0 else 1), h, x_send.at[h])
        for s in range(big_z - 1):

            @pl.when((z < big_z - 1) & (z - s >= 0))
            def _(s=s, h=h):
                pltpu.make_async_copy(piece(0, h), piece(0, h), z_send.at[h, 0, s]).wait()

            @pl.when((z > 0) & (z + s < big_z))
            def _(s=s, h=h):
                pltpu.make_async_copy(piece(0, h), piece(0, h), z_send.at[h, 1, s]).wait()


def gather_packed(parts, dims, halves, plan):
    big_z, big_y, big_x = dims
    rows, width, kind = sum(item[1] for item in halves), parts[-1].shape[1], parts[0].dtype
    count = big_z * big_y * big_x * 2
    dma = pltpu.SemaphoreType.DMA
    return pl.pallas_call(
        functools.partial(gather_kernel, dims, halves, plan),
        out_shape=jax.ShapeDtypeStruct((count, rows, width), kind),
        in_specs=[pl.BlockSpec(memory_space=pltpu.VMEM)] * len(parts),
        out_specs=pl.BlockSpec(memory_space=pl.ANY),
        scratch_shapes=[
            pltpu.VMEM((rows, width), kind),
            dma,
            dma((2, 2, max(big_z - 1, 1))),
            dma((2,)),
            dma((2,)),
            dma((2,)),
            dma((2, count)),
            dma((2,)),
        ],
        compiler_params=pltpu.CompilerParams(
            collective_id=0, has_side_effects=True, vmem_limit_bytes=VMEM_LIMIT
        ),
        name="gather_params",
    )(*parts)


def reduce_kernel(dims, halves, plan, *refs):
    parts, refs = refs[: len(plan)], refs[len(plan) :]
    out, grads, got_c, far_a, far_b, near_a, near_b, z_up, z_down = refs[:9]
    c_send, f_send, s_send, z_send, c_recv, fa_recv, fb_recv, sa_recv, sb_recv, z_recv = refs[9:]
    big_z, big_y, big_x = dims
    z, y, x, core = placement(dims)
    greet(dims, z, y, x, core)
    far, near = (far_a, far_b), (near_a, near_b)
    f_recv, s_recv = (fa_recv, fb_recv), (sa_recv, sb_recv)
    sizes = ((big_x, big_y), (big_y, big_x))
    mine = ((x, y), (y, x))

    def place(h, f, s, at):
        yy, xx = (s, f) if h == 0 else (f, s)
        return (at * big_y + yy) * big_x + xx

    def rows(h):
        return pl.ds(*halves[h])

    def await_(ref, sem):
        pltpu.make_async_copy(ref, ref, sem).wait()

    def target_f(h, f):
        return device_of(dims, z, y, f, core) if h == 0 else device_of(dims, z, f, x, core)

    def target_s(h, s):
        return device_of(dims, z, s, x, core) if h == 0 else device_of(dims, z, y, s, core)

    def send(src, dst, send_sem, recv_sem, target):
        pltpu.make_async_remote_copy(
            src_ref=src, dst_ref=dst, send_sem=send_sem, recv_sem=recv_sem,
            device_id=target, device_id_type=MESH,
        ).start()

    def each(step):
        for h in (0, 1):
            assert sizes[h][0] == sizes[1 - h][1]
        for df in list(range(1, max(big_x, big_y))) + [0]:
            for ds in list(range(1, max(big_x, big_y))) + [0]:

                @pl.loop(0, big_z)
                def _(t, df=df, ds=ds):
                    for h in (0, 1):
                        if df < sizes[h][0] and ds < sizes[h][1]:
                            f = (mine[h][0] + sizes[h][0] - df) % sizes[h][0]
                            s = (mine[h][1] + sizes[h][1] - ds) % sizes[h][1]
                            step(h, df, ds, f, s, t)

    def to_sibling(h, k):
        send(
            grads.at[2 * k + 1 - core, rows(h)], got_c.at[k, rows(h)],
            c_send.at[h], c_recv.at[h, k], device_of(dims, z, y, x, 1 - core),
        )

    def pack(i):
        for n, part in enumerate(parts):
            for first, count, column in plan[n]:
                grads[i, first : first + count, :] = part[i, :, column : column + grads.shape[2]]

    def pack_and_send(h, df, ds, f, s, t):
        i = 2 * place(h, f, s, t) + 1 - core
        if h == 0:
            pack(i)
            for half in (0, 1):
                to_sibling(half, i // 2)

    each(pack_and_send)

    @pl.loop(0, big_z * big_y * big_x)
    def _(k):
        pack(2 * k + core)

    def total(h, df, ds, f, s, t):
        k = place(h, f, s, t)
        await_(got_c.at[k, rows(h)], c_recv.at[h, k])
        value = grads[2 * k + core, rows(h)].astype(jnp.float32) + got_c[k, rows(h)].astype(
            jnp.float32
        )
        if df == 0:
            slot = s * big_z + t
            for d in range(sizes[h][0] - 1):
                await_(far[h].at[d, slot], f_recv[h].at[d, slot])
                value = value + far[h][d, slot].astype(jnp.float32)
            if ds == 0:
                for d in range(sizes[h][1] - 1):
                    await_(near[h].at[d, t], s_recv[h].at[d, t])
                    value = value + near[h][d, t].astype(jnp.float32)
        return 2 * k + core, value

    def forward(h, df, ds, f, s, t):
        if df == 0 and ds == 0:
            return
        k, value = total(h, df, ds, f, s, t)
        grads[k, rows(h)] = value.astype(grads.dtype)
        if df > 0:
            slot = s * big_z + t
            send(
                grads.at[k, rows(h)], far[h].at[df - 1, slot],
                f_send.at[h], f_recv[h].at[df - 1, slot], target_f(h, f),
            )
        else:
            send(
                grads.at[k, rows(h)], near[h].at[ds - 1, t],
                s_send.at[h], s_recv[h].at[ds - 1, t], target_s(h, s),
            )

    each(forward)

    for step in range(big_z - 1):
        for h in (0, 1):
            k_up, k_down = big_z - 1 - step, step

            @pl.when(z < k_up)
            def _(h=h, t=k_up):
                k, value = total(h, 0, 0, mine[h][0], mine[h][1], t)
                grads[k, rows(h)] = value.astype(grads.dtype)

                @pl.when(z > 0)
                def _():
                    await_(z_up.at[t, rows(h)], z_recv.at[h, 0, t])
                    grads[k, rows(h)] = (
                        grads[k, rows(h)].astype(jnp.float32) + z_up[t, rows(h)].astype(jnp.float32)
                    ).astype(grads.dtype)

                send(
                    grads.at[k, rows(h)], z_up.at[t, rows(h)], z_send.at[h, t],
                    z_recv.at[h, 0, t], device_of(dims, z + 1, y, x, core),
                )

            @pl.when(z > k_down)
            def _(h=h, t=k_down):
                k, value = total(h, 0, 0, mine[h][0], mine[h][1], t)
                grads[k, rows(h)] = value.astype(grads.dtype)

                @pl.when(z < big_z - 1)
                def _():
                    await_(z_down.at[t, rows(h)], z_recv.at[h, 1, t])
                    grads[k, rows(h)] = (
                        grads[k, rows(h)].astype(jnp.float32) + z_down[t, rows(h)].astype(jnp.float32)
                    ).astype(grads.dtype)

                send(
                    grads.at[k, rows(h)], z_down.at[t, rows(h)], z_send.at[h, t],
                    z_recv.at[h, 1, t], device_of(dims, z - 1, y, x, core),
                )

    for h in (0, 1):
        unused, value = total(h, 0, 0, mine[h][0], mine[h][1], z)
        out[rows(h)] = value

        @pl.when(z > 0)
        def _(h=h):
            await_(z_up.at[z, rows(h)], z_recv.at[h, 0, z])
            out[rows(h)] = out[rows(h)] + z_up[z, rows(h)].astype(jnp.float32)

        @pl.when(z < big_z - 1)
        def _(h=h):
            await_(z_down.at[z, rows(h)], z_recv.at[h, 1, z])
            out[rows(h)] = out[rows(h)] + z_down[z, rows(h)].astype(jnp.float32)

    def drain(count, h, sem):
        if count:
            await_(grads.at[pl.ds(0, count), rows(h)], sem)

    for h in (0, 1):
        drain(big_x * big_y * big_z, h, c_send.at[h])
        drain((sizes[h][0] - 1) * sizes[h][1] * big_z, h, f_send.at[h])
        drain((sizes[h][1] - 1) * big_z, h, s_send.at[h])
        for t in range(big_z):

            @pl.when(z != t)
            def _(h=h, t=t):
                await_(grads.at[0, rows(h)], z_send.at[h, t])


def reduce_packed(parts, dims, halves, plan):
    big_z, big_y, big_x = dims
    blocks = big_z * big_y * big_x
    rows, width, kind = sum(item[1] for item in halves), parts[-1].shape[2], parts[0].dtype
    dma = pltpu.SemaphoreType.DMA
    len_a, len_b = halves[0][1], halves[1][1]
    far_a = (max(big_x - 1, 1), big_y * big_z)
    far_b = (max(big_y - 1, 1), big_x * big_z)
    near_a = (max(big_y - 1, 1), big_z)
    near_b = (max(big_x - 1, 1), big_z)
    vmem = pl.BlockSpec(memory_space=pltpu.VMEM)
    return pl.pallas_call(
        functools.partial(reduce_kernel, dims, halves, plan),
        out_shape=jax.ShapeDtypeStruct((rows, width), jnp.float32),
        in_specs=[vmem] * len(parts),
        out_specs=vmem,
        scratch_shapes=[
            pltpu.VMEM((2 * blocks, rows, width), kind),
            pltpu.VMEM((blocks, rows, width), kind),
            pltpu.VMEM(far_a + (len_a, width), kind),
            pltpu.VMEM(far_b + (len_b, width), kind),
            pltpu.VMEM(near_a + (len_a, width), kind),
            pltpu.VMEM(near_b + (len_b, width), kind),
            pltpu.VMEM((big_z, rows, width), kind),
            pltpu.VMEM((big_z, rows, width), kind),
            dma((2,)),
            dma((2,)),
            dma((2,)),
            dma((2, big_z)),
            dma((2, blocks)),
            dma(far_a),
            dma(far_b),
            dma(near_a),
            dma(near_b),
            dma((2, 2, big_z)),
        ],
        compiler_params=pltpu.CompilerParams(
            collective_id=1, has_side_effects=True, vmem_limit_bytes=VMEM_LIMIT
        ),
        name="reduce_grads",
    )(*parts)


def normalize(values, gain_vec, shift_vec):
    centred = values - jnp.mean(values, axis=-1, keepdims=True)
    variance = jnp.mean(centred * centred, axis=-1, keepdims=True)
    return centred * lax.rsqrt(variance + EPSILON) * gain_vec + shift_vec


def heads_of(values):
    return values.reshape(values.shape[:-1] + (values.shape[-1] // HD, HD))


def shards(
    dims,
    layer_input,
    segments,
    cotangent,
    attend_weight,
    query_bias,
    value_bias,
    merge_weight,
    merge_bias,
    first_gain,
    first_shift,
    expand_weight,
    expand_bias,
    shrink_weight,
    shrink_bias,
    second_gain,
    second_shift,
):
    bfloat = jnp.bfloat16
    single = jnp.float32
    seq_count, block_width, features = layer_input.shape
    row_count = seq_count * block_width
    devices = dims[0] * dims[1] * dims[2] * 2
    depth = attend_weight.shape[0]
    wide = expand_weight.shape[1] // features
    narrow = shrink_weight.shape[0]

    def columns(values, parts):
        return [values[:, k * features : (k + 1) * features] for k in range(parts)]

    vectors = (
        query_bias, value_bias, merge_bias, first_gain, first_shift,
        shrink_bias, second_gain, second_shift, expand_bias,
    )
    used = sum(item.shape[0] for item in vectors)
    weight_rows = 3 * depth + depth + wide * depth + narrow
    pack_rows = -(-(weight_rows + 1 + seq_count) // 16) * 16
    first_half = pack_rows // 32 * 16
    halves = ((0, first_half), (first_half, pack_rows - first_half))
    vector_row = jnp.concatenate(vectors + (jnp.zeros((features - used,), bfloat),))[None]
    label_row = jnp.pad(segments.astype(bfloat), ((0, 0), (0, features - block_width)))
    vector_row = jnp.concatenate([vector_row, label_row])
    vector_row = jnp.pad(vector_row, ((0, pack_rows - weight_rows - 1 - seq_count), (0, 0)))
    plan = (
        tuple((k * depth, depth, k * features) for k in range(3)),
        ((3 * depth, depth, 0),),
        tuple(((4 + k) * depth, depth, k * features) for k in range(wide)),
        (((4 + wide) * depth, narrow, 0),),
        ((weight_rows, pack_rows - weight_rows, 0),),
    )
    gathered = gather_packed(
        (attend_weight, merge_weight, expand_weight, shrink_weight, vector_row), dims, halves, plan
    )

    def weight_at(first, count):
        return gathered[:, first : first + count].reshape(devices * count, features)

    group = 2 * dims[2]
    all_labels = lax.dynamic_slice_in_dim(
        gathered[:, weight_rows + 1 : weight_rows + 1 + seq_count, :block_width],
        lax.axis_index("dp") * group,
        group,
        0,
    )
    all_labels = jnp.swapaxes(all_labels, 0, 1).reshape(seq_count, group * block_width)
    all_labels = all_labels.astype(jnp.int32)
    w_attend = jnp.concatenate([weight_at(k * depth, depth) for k in range(3)], axis=1)
    w_merge = weight_at(3 * depth, depth)
    w_expand = jnp.concatenate([weight_at((4 + k) * depth, depth) for k in range(wide)], axis=1)
    w_shrink = weight_at((4 + wide) * depth, narrow)
    all_vectors = gathered[:, weight_rows].astype(single)
    spread, start = [], 0
    for item in vectors:
        spread.append(all_vectors[:, start : start + item.shape[0]].reshape(-1))
        start += item.shape[0]
    b_query, b_value, b_merge, g_first, s_first, b_shrink, g_second, s_second, b_expand = spread

    inputs = layer_input.astype(single).reshape(row_count, features)
    first_normed = normalize(inputs, g_first, s_first).astype(bfloat)
    project = jnp.dot(first_normed, w_attend, preferred_element_type=single)
    queries = ((project[:, :features] + b_query) * QUERY_SCALE).astype(bfloat)
    value_rows = project[:, 2 * features :] + b_value
    keys_values = jnp.concatenate([project[:, features : 2 * features], value_rows], axis=1).astype(
        bfloat
    )
    keys_values = keys_values.reshape(seq_count, block_width, 2 * features)
    all_keys_values = lax.all_gather(keys_values, "seq", axis=1, tiled=True)
    query_heads = heads_of(queries.reshape(seq_count, block_width, features))
    key_heads = heads_of(all_keys_values[..., :features])
    value_heads = heads_of(all_keys_values[..., features:])
    length = all_labels.shape[1]
    query_places = lax.axis_index("seq") * block_width + jnp.arange(block_width, dtype=jnp.int32)
    places = jnp.arange(length, dtype=jnp.int32)
    allowed = (places[None, None, :] <= query_places[None, :, None]) & (
        segments[:, :, None] == all_labels[:, None, :]
    )
    allowed = allowed[:, None]
    scores = jnp.einsum("sqhd,skhd->shqk", query_heads, key_heads, preferred_element_type=single)
    scores = jnp.where(allowed, scores, MASKED)
    peak = jnp.max(scores, axis=-1, keepdims=True)
    raised = jnp.where(allowed, jnp.exp(scores - peak), 0.0)
    probs = raised * (1.0 / jnp.sum(raised, axis=-1, keepdims=True))
    weights_low = probs.astype(bfloat)
    mixed = jnp.einsum(
        "shqk,skhd->sqhd", weights_low, value_heads, preferred_element_type=single
    )
    mixed = mixed.reshape(row_count, features).astype(bfloat)
    residual = inputs + jnp.dot(mixed, w_merge, preferred_element_type=single) + b_merge
    second_normed = normalize(residual, g_second, s_second).astype(bfloat)
    hidden_pre = jnp.dot(second_normed, w_expand, preferred_element_type=single) + b_expand
    hidden = jax.nn.gelu(hidden_pre).astype(bfloat)
    result = residual + jnp.dot(hidden, w_shrink, preferred_element_type=single) + b_shrink
    layer_output = result.astype(bfloat).reshape(seq_count, block_width, features)

    upstream_low = cotangent.reshape(row_count, features)
    upstream = upstream_low.astype(single)
    grad_shrink = jnp.einsum("rf,rd->fd", hidden, upstream_low, preferred_element_type=single)
    grad_shrink_bias = jnp.sum(upstream, axis=0)
    grad_hidden = jnp.einsum("rd,fd->rf", upstream_low, w_shrink, preferred_element_type=single)
    unused, gelu_pull = jax.vjp(jax.nn.gelu, hidden_pre)
    grad_pre = gelu_pull(grad_hidden)[0].astype(bfloat)
    grad_expand = jnp.einsum("rd,rf->df", second_normed, grad_pre, preferred_element_type=single)
    grad_expand_bias = jnp.sum(grad_pre.astype(single), axis=0)
    grad_second = jnp.einsum("rf,df->rd", grad_pre, w_expand, preferred_element_type=single)
    unused, second_pull = jax.vjp(normalize, residual, g_second, s_second)
    grad_res_norm, grad_second_gain, grad_second_shift = second_pull(grad_second)
    grad_res = upstream + grad_res_norm
    grad_branch = grad_res.astype(bfloat)
    grad_merge = jnp.einsum("rf,rd->fd", mixed, grad_branch, preferred_element_type=single)
    grad_merge_bias = jnp.sum(grad_branch.astype(single), axis=0)
    grad_mixed = jnp.einsum(
        "rd,fd->rf", grad_branch, w_merge, preferred_element_type=single
    ).astype(bfloat)
    grad_heads = heads_of(grad_mixed.reshape(seq_count, block_width, features))
    grad_probs = jnp.einsum("sqhd,skhd->shqk", grad_heads, value_heads, preferred_element_type=single)
    row_delta = jnp.sum(probs * grad_probs, axis=-1, keepdims=True)
    slopes = (probs * (grad_probs - row_delta)).astype(bfloat)
    grad_queries = jnp.einsum("shqk,skhd->sqhd", slopes, key_heads, preferred_element_type=single)
    grad_keys = jnp.einsum("shqk,sqhd->skhd", slopes, query_heads, preferred_element_type=single)
    grad_values = jnp.einsum(
        "shqk,sqhd->skhd", weights_low, grad_heads, preferred_element_type=single
    )
    grad_kv = jnp.concatenate(
        [
            grad_keys.reshape(seq_count, length, features),
            grad_values.reshape(seq_count, length, features),
        ],
        axis=-1,
    ).astype(bfloat)
    grad_kv_own = lax.psum_scatter(grad_kv, "seq", scatter_dimension=1, tiled=True)
    grad_kv_own = grad_kv_own.reshape(row_count, 2 * features)
    grad_query_low = grad_queries.astype(bfloat).reshape(row_count, features) * jnp.asarray(
        QUERY_SCALE, bfloat
    )
    grad_project = jnp.concatenate([grad_query_low, grad_kv_own], axis=-1)
    grad_attend = jnp.einsum("rd,rg->dg", first_normed, grad_project, preferred_element_type=single)
    grad_query_bias = jnp.sum(grad_query_low.astype(single), axis=0)
    grad_value_bias = jnp.sum(grad_kv_own[:, features:].astype(single), axis=0)
    grad_first = jnp.einsum("rg,dg->rd", grad_project, w_attend, preferred_element_type=single)
    unused, first_pull = jax.vjp(normalize, inputs, g_first, s_first)
    grad_in_norm, grad_first_gain, grad_first_shift = first_pull(grad_first)
    input_grad = (grad_res + grad_in_norm).reshape(seq_count, block_width, features)

    vector_grads = (
        grad_query_bias, grad_value_bias, grad_merge_bias, grad_first_gain, grad_first_shift,
        grad_shrink_bias, grad_second_gain, grad_second_shift, grad_expand_bias,
    )

    def blocks_of(values):
        low_values = values.astype(bfloat)
        return low_values.reshape(devices, low_values.shape[0] // devices, -1)

    vector_blocks = jnp.concatenate([blocks_of(item)[..., 0] for item in vector_grads], axis=1)
    vector_blocks = jnp.pad(
        vector_blocks[:, None], ((0, 0), (0, pack_rows - weight_rows - 1), (0, features - used))
    )
    parts = tuple(blocks_of(item) for item in (grad_attend, grad_merge, grad_expand, grad_shrink))
    parts = parts + (vector_blocks,)
    if depth % 8:
        one = jnp.concatenate(
            [
                part[..., column : column + features]
                for part, places_of in zip(parts, plan)
                for first, count, column in places_of
            ],
            axis=1,
        )
        parts, plan = (one,), (((0, pack_rows, 0),),)
    summed = reduce_packed(parts, dims, halves, plan)

    def side_by_side(first, parts):
        return jnp.concatenate(
            [summed[first + k * depth : first + (k + 1) * depth] for k in range(parts)], axis=1
        )

    vector_sums, start = [], 0
    for item in vectors:
        vector_sums.append(summed[weight_rows, start : start + item.shape[0]])
        start += item.shape[0]
    (
        query_sum, value_sum, merge_sum, gain_first_sum, shift_first_sum,
        shrink_sum, gain_second_sum, shift_second_sum, expand_sum,
    ) = vector_sums
    first_shrink = (4 + wide) * depth
    return (
        layer_output,
        input_grad,
        side_by_side(0, 3),
        query_sum,
        value_sum,
        summed[3 * depth : 4 * depth],
        merge_sum,
        gain_first_sum,
        shift_first_sum,
        side_by_side(4 * depth, wide),
        expand_sum,
        summed[first_shrink : first_shrink + narrow],
        shrink_sum,
        gain_second_sum,
        shift_second_sum,
    )


def solution(mesh):
    across = mesh.shape["seq"] // 2
    dims = (mesh.shape["dp"] // across, across, across)
    placed = (
        P("dp", "seq", None),
        P("dp", "seq"),
        P("dp", "seq", None),
        P(("dp", "seq"), None),
        P(("dp", "seq")),
        P(("dp", "seq")),
        P(("dp", "seq"), None),
        P(("dp", "seq")),
        P(("dp", "seq")),
        P(("dp", "seq")),
        P(("dp", "seq"), None),
        P(("dp", "seq")),
        P(("dp", "seq"), None),
        P(("dp", "seq")),
        P(("dp", "seq")),
        P(("dp", "seq")),
    )
    return jax.shard_map(
        functools.partial(shards, dims),
        mesh=mesh,
        in_specs=placed,
        out_specs=(
            P("dp", "seq", None),
            P("dp", "seq", None),
            P(("dp", "seq"), None),
            P(("dp", "seq")),
            P(("dp", "seq")),
            P(("dp", "seq"), None),
            P(("dp", "seq")),
            P(("dp", "seq")),
            P(("dp", "seq")),
            P(("dp", "seq"), None),
            P(("dp", "seq")),
            P(("dp", "seq"), None),
            P(("dp", "seq")),
            P(("dp", "seq")),
            P(("dp", "seq")),
        ),
        check_vma=False,
    )
```

```python
import functools

import jax
import jax.numpy as jnp
from jax import lax
from jax.experimental import pallas as pl
from jax.experimental.pallas import tpu as pltpu
from jax.sharding import PartitionSpec as P

HD = 64
EPSILON = 1e-05
MASKED = -1e30
QUERY_SCALE = 0.125
MESH = pl.DeviceIdType.MESH
VMEM_LIMIT = 58 * 1024 * 1024


def placement(dims):
    big_y = dims[1]
    dp, seq = lax.axis_index("dp"), lax.axis_index("seq")
    return dp // big_y, dp % big_y, seq // 2, seq % 2


def device_of(dims, z, y, x, core):
    return (z * dims[1] + y, x * 2 + core)


def owner_of(dims, z, y, x, core):
    return (z * dims[1] + y) * (2 * dims[2]) + x * 2 + core


def greet(dims, z, y, x, core):
    big_z, big_y, big_x = dims
    barrier = pltpu.get_barrier_semaphore()

    def signal(target):
        pl.semaphore_signal(barrier, inc=1, device_id=target, device_id_type=MESH)

    @pl.when(z > 0)
    def _():
        signal(device_of(dims, z - 1, y, x, core))

    @pl.when(z < big_z - 1)
    def _():
        signal(device_of(dims, z + 1, y, x, core))

    for d in range(1, big_y):
        signal(device_of(dims, z, (y + d) % big_y, x, core))
    for d in range(1, big_x):
        signal(device_of(dims, z, y, (x + d) % big_x, core))
    signal(device_of(dims, z, y, x, 1 - core))
    along_z = (z + big_z - 1) // big_z + (big_z - 1 - z + big_z - 1) // big_z
    pl.semaphore_wait(barrier, big_y - 1 + big_x - 1 + 1 + along_z)


def gather_kernel(
    dims, halves, plan, attend, merge, expand, shrink, vectors, out, src, own_sem,
    z_send, y_send, x_send, c_send, recv, c_recv,
):
    big_z, big_y, big_x = dims
    z, y, x, core = placement(dims)
    me = owner_of(dims, z, y, x, core)
    for k, part in enumerate((attend, merge, expand, shrink, vectors)):
        for first, count, column in plan[k]:
            src[first : first + count, :] = part[:, column : column + src.shape[1]]
    greet(dims, z, y, x, core)
    own = pltpu.make_async_copy(src, out.at[me], own_sem)
    own.start()

    def piece(i, h):
        return out.at[i, pl.ds(*halves[h])]

    def send(i, h, target, send_sem, recv_sem, mine=False):
        pltpu.make_async_remote_copy(
            src_ref=src.at[pl.ds(*halves[h])] if mine else piece(i, h),
            dst_ref=piece(i, h),
            send_sem=send_sem,
            recv_sem=recv_sem,
            device_id=target,
            device_id_type=MESH,
        ).start()

    def arrived(i, h):
        pltpu.make_async_copy(piece(i, h), piece(i, h), recv.at[h, i]).wait()

    def to_y(i, h, mine=False):
        for d in range(1, big_y):
            target = device_of(dims, z, (y + d) % big_y, x, core)
            send(i, h, target, y_send.at[h], recv.at[h, i], mine)

    def to_x(i, h, mine=False):
        for d in range(1, big_x):
            target = device_of(dims, z, y, (x + d) % big_x, core)
            send(i, h, target, x_send.at[h], recv.at[h, i], mine)

    def to_core(i, h, mine=False):
        send(i, h, device_of(dims, z, y, x, 1 - core), c_send.at[h], c_recv.at[h], mine)

    def up(i, h, s, mine=False):
        @pl.when(z < big_z - 1)
        def _():
            send(i, h, device_of(dims, z + 1, y, x, core), z_send.at[h, 0, s], recv.at[h, i], mine)

    def down(i, h, s, mine=False):
        @pl.when(z > 0)
        def _():
            send(i, h, device_of(dims, z - 1, y, x, core), z_send.at[h, 1, s], recv.at[h, i], mine)

    def fan(i, h, mine=False):
        for go in (to_y, to_x) if h == 0 else (to_x, to_y):
            go(i, h, mine)
        to_core(i, h, mine)

    for h in (0, 1):
        up(me, h, 0, True)
        down(me, h, 0, True)
        fan(me, h, True)

    for s in range(1, big_z):
        for h in (0, 1):

            @pl.when(z - s >= 0)
            def _(s=s, h=h):
                i = owner_of(dims, z - s, y, x, core)
                arrived(i, h)
                if s < big_z - 1:
                    up(i, h, s)
                fan(i, h)

            @pl.when(z + s < big_z)
            def _(s=s, h=h):
                i = owner_of(dims, z + s, y, x, core)
                arrived(i, h)
                if s < big_z - 1:
                    down(i, h, s)
                fan(i, h)

    @pl.loop(0, big_z)
    def _(s):
        at = (z + s) % big_z
        for d in range(1, big_y):
            i = owner_of(dims, at, (y + d) % big_y, x, core)
            arrived(i, 0)
            to_x(i, 0)
            to_core(i, 0)
        for d in range(1, big_x):
            i = owner_of(dims, at, y, (x + d) % big_x, core)
            arrived(i, 1)
            to_y(i, 1)
            to_core(i, 1)

    for e in range(max(big_x, big_y)):

        @pl.loop(0, big_z)
        def _(s, e=e):
            at = (z + s) % big_z
            if e < big_y:
                for d in range(1, big_x):
                    i = owner_of(dims, at, (y + e) % big_y, (x + d) % big_x, core)
                    arrived(i, 0)
                    to_core(i, 0)
            if e < big_x:
                for d in range(1, big_y):
                    i = owner_of(dims, at, (y + d) % big_y, (x + e) % big_x, core)
                    arrived(i, 1)
                    to_core(i, 1)

    def drain(count, h, sem):
        if count:
            region = out.at[pl.ds(0, count), pl.ds(*halves[h])]
            pltpu.make_async_copy(region, region, sem).wait()

    own.wait()
    for h in (0, 1):
        drain(big_x * big_y * big_z, h, c_recv.at[h])
        drain(big_x * big_y * big_z, h, c_send.at[h])
        drain((big_y - 1) * big_z * (1 if h == 0 else big_x), h, y_send.at[h])
        drain((big_x - 1) * big_z * (big_y if h == 0 else 1), h, x_send.at[h])
        for s in range(big_z - 1):

            @pl.when((z < big_z - 1) & (z - s >= 0))
            def _(s=s, h=h):
                pltpu.make_async_copy(piece(0, h), piece(0, h), z_send.at[h, 0, s]).wait()

            @pl.when((z > 0) & (z + s < big_z))
            def _(s=s, h=h):
                pltpu.make_async_copy(piece(0, h), piece(0, h), z_send.at[h, 1, s]).wait()


def gather_packed(parts, dims, halves, plan):
    big_z, big_y, big_x = dims
    rows, width, kind = sum(item[1] for item in halves), parts[-1].shape[1], parts[0].dtype
    count = big_z * big_y * big_x * 2
    dma = pltpu.SemaphoreType.DMA
    return pl.pallas_call(
        functools.partial(gather_kernel, dims, halves, plan),
        out_shape=jax.ShapeDtypeStruct((count, rows, width), kind),
        in_specs=[pl.BlockSpec(memory_space=pltpu.VMEM)] * len(parts),
        out_specs=pl.BlockSpec(memory_space=pl.ANY),
        scratch_shapes=[
            pltpu.VMEM((rows, width), kind),
            dma,
            dma((2, 2, max(big_z - 1, 1))),
            dma((2,)),
            dma((2,)),
            dma((2,)),
            dma((2, count)),
            dma((2,)),
        ],
        compiler_params=pltpu.CompilerParams(
            collective_id=0, has_side_effects=True, vmem_limit_bytes=VMEM_LIMIT
        ),
        name="gather_params",
    )(*parts)


def reduce_kernel(dims, halves, plan, *refs):
    parts, refs = refs[: len(plan)], refs[len(plan) :]
    out, grads, got_c, far_a, far_b, near_a, near_b, z_up, z_down = refs[:9]
    c_send, f_send, s_send, z_send, c_recv, fa_recv, fb_recv, sa_recv, sb_recv, z_recv = refs[9:]
    big_z, big_y, big_x = dims
    z, y, x, core = placement(dims)
    greet(dims, z, y, x, core)
    far, near = (far_a, far_b), (near_a, near_b)
    f_recv, s_recv = (fa_recv, fb_recv), (sa_recv, sb_recv)
    sizes = ((big_x, big_y), (big_y, big_x))
    mine = ((x, y), (y, x))

    def place(h, f, s, at):
        yy, xx = (s, f) if h == 0 else (f, s)
        return (at * big_y + yy) * big_x + xx

    def rows(h):
        return pl.ds(*halves[h])

    def await_(ref, sem):
        pltpu.make_async_copy(ref, ref, sem).wait()

    def target_f(h, f):
        return device_of(dims, z, y, f, core) if h == 0 else device_of(dims, z, f, x, core)

    def target_s(h, s):
        return device_of(dims, z, s, x, core) if h == 0 else device_of(dims, z, y, s, core)

    def send(src, dst, send_sem, recv_sem, target):
        pltpu.make_async_remote_copy(
            src_ref=src, dst_ref=dst, send_sem=send_sem, recv_sem=recv_sem,
            device_id=target, device_id_type=MESH,
        ).start()

    def to_sibling(h, k):
        send(
            grads.at[2 * k + 1 - core, rows(h)], got_c.at[k, rows(h)],
            c_send.at[h], c_recv.at[h, k], device_of(dims, z, y, x, 1 - core),
        )

    def pack(i):
        for n, part in enumerate(parts):
            for first, count, column in plan[n]:
                grads[i, first : first + count, :] = part[i, :, column : column + grads.shape[2]]

    def prepare(t):
        @pl.loop(1, big_y * big_x + 1)
        def _(j):
            yy, xx = (y + j // big_x) % big_y, (x + j) % big_x
            k = (t * big_y + yy) * big_x + xx
            pack(2 * k + 1 - core)
            for h in (0, 1):
                to_sibling(h, k)
            pack(2 * k + core)

    def total(h, df, ds, f, s, t):
        k = place(h, f, s, t)
        await_(got_c.at[k, rows(h)], c_recv.at[h, k])
        value = grads[2 * k + core, rows(h)].astype(jnp.float32) + got_c[k, rows(h)].astype(
            jnp.float32
        )
        if df == 0:
            slot = s * big_z + t
            for d in range(sizes[h][0] - 1):
                await_(far[h].at[d, slot], f_recv[h].at[d, slot])
                value = value + far[h][d, slot].astype(jnp.float32)
            if ds == 0:
                for d in range(sizes[h][1] - 1):
                    await_(near[h].at[d, t], s_recv[h].at[d, t])
                    value = value + near[h][d, t].astype(jnp.float32)
        return 2 * k + core, value

    def to_far(t):
        for df in range(1, big_x):

            @pl.loop(1, big_y + 1)
            def _(ds):
                for h in (0, 1):
                    f, s = (mine[h][0] + big_x - df) % big_x, (mine[h][1] + ds) % big_y
                    k, value = total(h, df, None, f, s, t)
                    grads[k, rows(h)] = value.astype(grads.dtype)
                    slot = s * big_z + t
                    send(
                        grads.at[k, rows(h)], far[h].at[df - 1, slot],
                        f_send.at[h], f_recv[h].at[df - 1, slot], target_f(h, f),
                    )

    def to_near(t):
        for ds in range(1, big_y):
            for h in (0, 1):
                f, s = mine[h][0], (mine[h][1] + big_y - ds) % big_y
                k, value = total(h, 0, ds, f, s, t)
                grads[k, rows(h)] = value.astype(grads.dtype)
                send(
                    grads.at[k, rows(h)], near[h].at[ds - 1, t],
                    s_send.at[h], s_recv[h].at[ds - 1, t], target_s(h, s),
                )

    def along_line(t):
        for h in (0, 1):
            for side, passed, sends, first, ahead in (
                (0, z_up, z < t, z > 0, 1),
                (1, z_down, z > t, z < big_z - 1, -1),
            ):

                @pl.when(sends)
                def _(h=h, side=side, passed=passed, first=first, ahead=ahead):
                    k, value = total(h, 0, 0, mine[h][0], mine[h][1], t)
                    grads[k, rows(h)] = value.astype(grads.dtype)

                    @pl.when(first)
                    def _():
                        await_(passed.at[t, rows(h)], z_recv.at[h, side, t])
                        grads[k, rows(h)] = (
                            grads[k, rows(h)].astype(jnp.float32)
                            + passed[t, rows(h)].astype(jnp.float32)
                        ).astype(grads.dtype)

                    send(
                        grads.at[k, rows(h)], passed.at[t, rows(h)], z_send.at[h, t],
                        z_recv.at[h, side, t], device_of(dims, z + ahead, y, x, core),
                    )

    order = sorted(range(big_z), key=lambda t: (-abs(2 * t - big_z + 1), -t))
    for u in range(big_z + 4):
        for stage, lag in ((prepare, 0), (to_far, 1), (to_near, 3), (along_line, 4)):
            if 0 <= u - lag < big_z:
                stage(order[u - lag])

    for h in (0, 1):
        unused, value = total(h, 0, 0, mine[h][0], mine[h][1], z)
        out[rows(h)] = value

        @pl.when(z > 0)
        def _(h=h):
            await_(z_up.at[z, rows(h)], z_recv.at[h, 0, z])
            out[rows(h)] = out[rows(h)] + z_up[z, rows(h)].astype(jnp.float32)

        @pl.when(z < big_z - 1)
        def _(h=h):
            await_(z_down.at[z, rows(h)], z_recv.at[h, 1, z])
            out[rows(h)] = out[rows(h)] + z_down[z, rows(h)].astype(jnp.float32)

    def drain(count, h, sem):
        if count:
            await_(grads.at[pl.ds(0, count), rows(h)], sem)

    for h in (0, 1):
        drain(big_x * big_y * big_z, h, c_send.at[h])
        drain((sizes[h][0] - 1) * sizes[h][1] * big_z, h, f_send.at[h])
        drain((sizes[h][1] - 1) * big_z, h, s_send.at[h])
        for t in range(big_z):

            @pl.when(z != t)
            def _(h=h, t=t):
                await_(grads.at[0, rows(h)], z_send.at[h, t])


def reduce_packed(parts, dims, halves, plan):
    big_z, big_y, big_x = dims
    blocks = big_z * big_y * big_x
    rows, width, kind = sum(item[1] for item in halves), parts[-1].shape[2], parts[0].dtype
    dma = pltpu.SemaphoreType.DMA
    len_a, len_b = halves[0][1], halves[1][1]
    far_a = (max(big_x - 1, 1), big_y * big_z)
    far_b = (max(big_y - 1, 1), big_x * big_z)
    near_a = (max(big_y - 1, 1), big_z)
    near_b = (max(big_x - 1, 1), big_z)
    vmem = pl.BlockSpec(memory_space=pltpu.VMEM)
    return pl.pallas_call(
        functools.partial(reduce_kernel, dims, halves, plan),
        out_shape=jax.ShapeDtypeStruct((rows, width), jnp.float32),
        in_specs=[vmem] * len(parts),
        out_specs=vmem,
        scratch_shapes=[
            pltpu.VMEM((2 * blocks, rows, width), kind),
            pltpu.VMEM((blocks, rows, width), kind),
            pltpu.VMEM(far_a + (len_a, width), kind),
            pltpu.VMEM(far_b + (len_b, width), kind),
            pltpu.VMEM(near_a + (len_a, width), kind),
            pltpu.VMEM(near_b + (len_b, width), kind),
            pltpu.VMEM((big_z, rows, width), kind),
            pltpu.VMEM((big_z, rows, width), kind),
            dma((2,)),
            dma((2,)),
            dma((2,)),
            dma((2, big_z)),
            dma((2, blocks)),
            dma(far_a),
            dma(far_b),
            dma(near_a),
            dma(near_b),
            dma((2, 2, big_z)),
        ],
        compiler_params=pltpu.CompilerParams(
            collective_id=1, has_side_effects=True, vmem_limit_bytes=VMEM_LIMIT
        ),
        name="reduce_grads",
    )(*parts)


def normalize(values, gain_vec, shift_vec):
    centred = values - jnp.mean(values, axis=-1, keepdims=True)
    variance = jnp.mean(centred * centred, axis=-1, keepdims=True)
    return centred * lax.rsqrt(variance + EPSILON) * gain_vec + shift_vec


def heads_of(values):
    return values.reshape(values.shape[:-1] + (values.shape[-1] // HD, HD))


def shards(
    dims,
    layer_input,
    segments,
    cotangent,
    attend_weight,
    query_bias,
    value_bias,
    merge_weight,
    merge_bias,
    first_gain,
    first_shift,
    expand_weight,
    expand_bias,
    shrink_weight,
    shrink_bias,
    second_gain,
    second_shift,
):
    bfloat = jnp.bfloat16
    single = jnp.float32
    seq_count, block_width, features = layer_input.shape
    row_count = seq_count * block_width
    devices = dims[0] * dims[1] * dims[2] * 2
    depth = attend_weight.shape[0]
    wide = expand_weight.shape[1] // features
    narrow = shrink_weight.shape[0]

    def columns(values, parts):
        return [values[:, k * features : (k + 1) * features] for k in range(parts)]

    vectors = (
        query_bias, value_bias, merge_bias, first_gain, first_shift,
        shrink_bias, second_gain, second_shift, expand_bias,
    )
    used = sum(item.shape[0] for item in vectors)
    weight_rows = 3 * depth + depth + wide * depth + narrow
    pack_rows = -(-(weight_rows + 1 + seq_count) // 16) * 16
    first_half = pack_rows // 32 * 16
    halves = ((0, first_half), (first_half, pack_rows - first_half))
    vector_row = jnp.concatenate(vectors + (jnp.zeros((features - used,), bfloat),))[None]
    label_row = jnp.pad(segments.astype(bfloat), ((0, 0), (0, features - block_width)))
    vector_row = jnp.concatenate([vector_row, label_row])
    vector_row = jnp.pad(vector_row, ((0, pack_rows - weight_rows - 1 - seq_count), (0, 0)))
    plan = (
        tuple((k * depth, depth, k * features) for k in range(3)),
        ((3 * depth, depth, 0),),
        tuple(((4 + k) * depth, depth, k * features) for k in range(wide)),
        (((4 + wide) * depth, narrow, 0),),
        ((weight_rows, pack_rows - weight_rows, 0),),
    )
    gathered = gather_packed(
        (attend_weight, merge_weight, expand_weight, shrink_weight, vector_row), dims, halves, plan
    )

    def weight_at(first, count):
        return gathered[:, first : first + count].reshape(devices * count, features)

    group = 2 * dims[2]
    all_labels = lax.dynamic_slice_in_dim(
        gathered[:, weight_rows + 1 : weight_rows + 1 + seq_count, :block_width],
        lax.axis_index("dp") * group,
        group,
        0,
    )
    all_labels = jnp.swapaxes(all_labels, 0, 1).reshape(seq_count, group * block_width)
    all_labels = all_labels.astype(jnp.int32)
    w_attend = jnp.concatenate([weight_at(k * depth, depth) for k in range(3)], axis=1)
    w_merge = weight_at(3 * depth, depth)
    w_expand = jnp.concatenate([weight_at((4 + k) * depth, depth) for k in range(wide)], axis=1)
    w_shrink = weight_at((4 + wide) * depth, narrow)
    all_vectors = gathered[:, weight_rows].astype(single)
    spread, start = [], 0
    for item in vectors:
        spread.append(all_vectors[:, start : start + item.shape[0]].reshape(-1))
        start += item.shape[0]
    b_query, b_value, b_merge, g_first, s_first, b_shrink, g_second, s_second, b_expand = spread

    inputs = layer_input.astype(single).reshape(row_count, features)
    first_normed = normalize(inputs, g_first, s_first).astype(bfloat)
    project = jnp.dot(first_normed, w_attend, preferred_element_type=single)
    queries = ((project[:, :features] + b_query) * QUERY_SCALE).astype(bfloat)
    value_rows = project[:, 2 * features :] + b_value
    keys_values = jnp.concatenate([project[:, features : 2 * features], value_rows], axis=1).astype(
        bfloat
    )
    keys_values = keys_values.reshape(seq_count, block_width, 2 * features)
    all_keys_values = lax.all_gather(keys_values, "seq", axis=1, tiled=True)
    query_heads = heads_of(queries.reshape(seq_count, block_width, features))
    key_heads = heads_of(all_keys_values[..., :features])
    value_heads = heads_of(all_keys_values[..., features:])
    length = all_labels.shape[1]
    query_places = lax.axis_index("seq") * block_width + jnp.arange(block_width, dtype=jnp.int32)
    places = jnp.arange(length, dtype=jnp.int32)
    allowed = (places[None, None, :] <= query_places[None, :, None]) & (
        segments[:, :, None] == all_labels[:, None, :]
    )
    allowed = allowed[:, None]
    scores = jnp.einsum("sqhd,skhd->shqk", query_heads, key_heads, preferred_element_type=single)
    scores = jnp.where(allowed, scores, MASKED)
    peak = jnp.max(scores, axis=-1, keepdims=True)
    raised = jnp.where(allowed, jnp.exp(scores - peak), 0.0)
    probs = raised * (1.0 / jnp.sum(raised, axis=-1, keepdims=True))
    weights_low = probs.astype(bfloat)
    mixed = jnp.einsum(
        "shqk,skhd->sqhd", weights_low, value_heads, preferred_element_type=single
    )
    mixed = mixed.reshape(row_count, features).astype(bfloat)
    residual = inputs + jnp.dot(mixed, w_merge, preferred_element_type=single) + b_merge
    second_normed = normalize(residual, g_second, s_second).astype(bfloat)
    hidden_pre = jnp.dot(second_normed, w_expand, preferred_element_type=single) + b_expand
    hidden = jax.nn.gelu(hidden_pre).astype(bfloat)
    result = residual + jnp.dot(hidden, w_shrink, preferred_element_type=single) + b_shrink
    layer_output = result.astype(bfloat).reshape(seq_count, block_width, features)

    upstream_low = cotangent.reshape(row_count, features)
    upstream = upstream_low.astype(single)
    grad_shrink = jnp.einsum("rf,rd->fd", hidden, upstream_low, preferred_element_type=single)
    grad_shrink_bias = jnp.sum(upstream, axis=0)
    grad_hidden = jnp.einsum("rd,fd->rf", upstream_low, w_shrink, preferred_element_type=single)
    unused, gelu_pull = jax.vjp(jax.nn.gelu, hidden_pre)
    grad_pre = gelu_pull(grad_hidden)[0].astype(bfloat)
    grad_expand = jnp.einsum("rd,rf->df", second_normed, grad_pre, preferred_element_type=single)
    grad_expand_bias = jnp.sum(grad_pre.astype(single), axis=0)
    grad_second = jnp.einsum("rf,df->rd", grad_pre, w_expand, preferred_element_type=single)
    unused, second_pull = jax.vjp(normalize, residual, g_second, s_second)
    grad_res_norm, grad_second_gain, grad_second_shift = second_pull(grad_second)
    grad_res = upstream + grad_res_norm
    grad_branch = grad_res.astype(bfloat)
    grad_merge = jnp.einsum("rf,rd->fd", mixed, grad_branch, preferred_element_type=single)
    grad_merge_bias = jnp.sum(grad_branch.astype(single), axis=0)
    grad_mixed = jnp.einsum(
        "rd,fd->rf", grad_branch, w_merge, preferred_element_type=single
    ).astype(bfloat)
    grad_heads = heads_of(grad_mixed.reshape(seq_count, block_width, features))
    grad_probs = jnp.einsum("sqhd,skhd->shqk", grad_heads, value_heads, preferred_element_type=single)
    row_delta = jnp.sum(probs * grad_probs, axis=-1, keepdims=True)
    slopes = (probs * (grad_probs - row_delta)).astype(bfloat)
    grad_queries = jnp.einsum("shqk,skhd->sqhd", slopes, key_heads, preferred_element_type=single)
    grad_keys = jnp.einsum("shqk,sqhd->skhd", slopes, query_heads, preferred_element_type=single)
    grad_values = jnp.einsum(
        "shqk,sqhd->skhd", weights_low, grad_heads, preferred_element_type=single
    )
    grad_kv = jnp.concatenate(
        [
            grad_keys.reshape(seq_count, length, features),
            grad_values.reshape(seq_count, length, features),
        ],
        axis=-1,
    ).astype(bfloat)
    grad_kv_own = lax.psum_scatter(grad_kv, "seq", scatter_dimension=1, tiled=True)
    grad_kv_own = grad_kv_own.reshape(row_count, 2 * features)
    grad_query_low = grad_queries.astype(bfloat).reshape(row_count, features) * jnp.asarray(
        QUERY_SCALE, bfloat
    )
    grad_project = jnp.concatenate([grad_query_low, grad_kv_own], axis=-1)
    grad_attend = jnp.einsum("rd,rg->dg", first_normed, grad_project, preferred_element_type=single)
    grad_query_bias = jnp.sum(grad_query_low.astype(single), axis=0)
    grad_value_bias = jnp.sum(grad_kv_own[:, features:].astype(single), axis=0)
    grad_first = jnp.einsum("rg,dg->rd", grad_project, w_attend, preferred_element_type=single)
    unused, first_pull = jax.vjp(normalize, inputs, g_first, s_first)
    grad_in_norm, grad_first_gain, grad_first_shift = first_pull(grad_first)
    input_grad = (grad_res + grad_in_norm).reshape(seq_count, block_width, features)

    vector_grads = (
        grad_query_bias, grad_value_bias, grad_merge_bias, grad_first_gain, grad_first_shift,
        grad_shrink_bias, grad_second_gain, grad_second_shift, grad_expand_bias,
    )

    def blocks_of(values):
        low_values = values.astype(bfloat)
        return low_values.reshape(devices, low_values.shape[0] // devices, -1)

    vector_blocks = jnp.concatenate([blocks_of(item)[..., 0] for item in vector_grads], axis=1)
    vector_blocks = jnp.pad(
        vector_blocks[:, None], ((0, 0), (0, pack_rows - weight_rows - 1), (0, features - used))
    )
    parts = tuple(blocks_of(item) for item in (grad_attend, grad_merge, grad_expand, grad_shrink))
    parts = parts + (vector_blocks,)
    if depth % 8:
        one = jnp.concatenate(
            [
                part[..., column : column + features]
                for part, places_of in zip(parts, plan)
                for first, count, column in places_of
            ],
            axis=1,
        )
        parts, plan = (one,), (((0, pack_rows, 0),),)
    summed = reduce_packed(parts, dims, halves, plan)

    def side_by_side(first, parts):
        return jnp.concatenate(
            [summed[first + k * depth : first + (k + 1) * depth] for k in range(parts)], axis=1
        )

    vector_sums, start = [], 0
    for item in vectors:
        vector_sums.append(summed[weight_rows, start : start + item.shape[0]])
        start += item.shape[0]
    (
        query_sum, value_sum, merge_sum, gain_first_sum, shift_first_sum,
        shrink_sum, gain_second_sum, shift_second_sum, expand_sum,
    ) = vector_sums
    first_shrink = (4 + wide) * depth
    return (
        layer_output,
        input_grad,
        side_by_side(0, 3),
        query_sum,
        value_sum,
        summed[3 * depth : 4 * depth],
        merge_sum,
        gain_first_sum,
        shift_first_sum,
        side_by_side(4 * depth, wide),
        expand_sum,
        summed[first_shrink : first_shrink + narrow],
        shrink_sum,
        gain_second_sum,
        shift_second_sum,
    )


def solution(mesh):
    across = mesh.shape["seq"] // 2
    dims = (mesh.shape["dp"] // across, across, across)
    placed = (
        P("dp", "seq", None),
        P("dp", "seq"),
        P("dp", "seq", None),
        P(("dp", "seq"), None),
        P(("dp", "seq")),
        P(("dp", "seq")),
        P(("dp", "seq"), None),
        P(("dp", "seq")),
        P(("dp", "seq")),
        P(("dp", "seq")),
        P(("dp", "seq"), None),
        P(("dp", "seq")),
        P(("dp", "seq"), None),
        P(("dp", "seq")),
        P(("dp", "seq")),
        P(("dp", "seq")),
    )
    return jax.shard_map(
        functools.partial(shards, dims),
        mesh=mesh,
        in_specs=placed,
        out_specs=(
            P("dp", "seq", None),
            P("dp", "seq", None),
            P(("dp", "seq"), None),
            P(("dp", "seq")),
            P(("dp", "seq")),
            P(("dp", "seq"), None),
            P(("dp", "seq")),
            P(("dp", "seq")),
            P(("dp", "seq")),
            P(("dp", "seq"), None),
            P(("dp", "seq")),
            P(("dp", "seq"), None),
            P(("dp", "seq")),
            P(("dp", "seq")),
            P(("dp", "seq")),
        ),
        check_vma=False,
    )
```
